128 devices in a mesh: lat: 8 (over x_hi, y), lon: 16 (over x_lo, z, core).
Axes of the slice: x: 4 (x_hi: 2, x_lo: 2; x = x_hi * 2 + x_lo), y: 4, z: 4, core: 2. Of those that a mesh axis runs over, the one named last changes fastest.
Arguments:
- tokens: bfloat16 [3, 96, 384, 512], P(None, 'lat', 'lon'), may hold values from -6 to 6
- region_ids: int32 [96, 384], replicated, may hold values from 0 to 15, as said below
- w_qkv: bfloat16 [2, 512, 1536], replicated, may hold values from -0.30935922 to 0.30935922
- w_proj: bfloat16 [2, 512, 512], replicated, may hold values from -0.25 to 0.25
- w_up: bfloat16 [2, 512, 2048], replicated, may hold values from -0.25 to 0.25
- w_down: bfloat16 [2, 2048, 512], replicated, may hold values from -0.125 to 0.125
- merge_first: bfloat16 [2048, 1024], replicated, may hold values from -0.125 to 0.125
- merge_second: bfloat16 [4096, 2048], P(None, 'lon'), may hold values from -0.09375 to 0.09375
Outputs:
- fine: bfloat16 [3, 96, 384, 512], P(None, 'lat', 'lon')
- coarse: bfloat16 [3, 24, 96, 2048], P(None, 'lat', 'lon')
The draws below stay inside these ranges and needn't reach their ends.
Inputs may be any that keep to these rules, and one draw needn't show every extreme that they name: `region_ids`: regions are rectangles: latitude rows fall into contiguous bands and longitude columns into contiguous bands, and a cell's id is 4 times its latitude band's number modulo 4 plus its longitude band's number modulo 4. A band begins only at row or column 0 or at an index that is not a multiple of 3.
All inputs are finite; a program needn't handle non-finite values.
Results may differ from the reference program's by a relative error of at most 0.025.
Values may be sent and summed in bfloat16 or wider, within the bound.
A program may use at most 192 MiB of HBM per device.

```python
import jax
import jax.numpy as jnp
from jax import lax

D = 512
HEADS = 8
LEV = 3
WIN_LAT = 6
WIN_LON = 12
SHIFT_LAT = 3
SHIFT_LON = 6
FF = 2048
NLAT = 96
NLON = 384


def draw_w_qkv(key, part):
    key = jax.random.fold_in(key, 7)
    values = jnp.clip(jax.random.normal(key, (2, D, 3 * D), jnp.float32), -6.0, 6.0) * D ** (-0.5)
    return values.astype(jnp.bfloat16)


def band_numbers(key, count):
    position = jnp.arange(count, dtype=jnp.int32)
    allowed = (position % 3 != 0).astype(jnp.int32)
    random_edges = (jax.random.randint(key, (count,), 0, 6) == 0).astype(jnp.int32) * allowed
    forced_edges = ((position == 2) | (position == 8) | (position == 16)).astype(jnp.int32)
    edges = jnp.where(position == 0, 0, jnp.maximum(random_edges, forced_edges))
    return jnp.cumsum(edges).astype(jnp.int32) % 4


def draw_region_ids(key, part):
    key = jax.random.fold_in(key, 11)
    row_key, col_key = jax.random.split(key)
    row_bands = band_numbers(row_key, NLAT)
    col_bands = band_numbers(col_key, NLON)
    return (row_bands[:, None] * 4 + col_bands[None, :]).astype(jnp.int32)


def block_levels(stream_key, extent, cuts, low, largest):
    def one(dim, parts):
        steps = jax.random.uniform(jax.random.fold_in(jax.random.fold_in(stream_key, 6), dim), (parts,), jnp.float32, low / len(cuts), largest / len(cuts))
        return jnp.repeat(jnp.exp(steps), extent[dim] // parts).reshape((-1,) + (1,) * (len(extent) - dim - 1))

    factor_of = one(*cuts[0])
    for cut in cuts[1:]:
        factor_of = factor_of * one(*cut)
    return factor_of


def scatter_about(own_key, dims, width, reach, cuts=(), kind=jnp.bfloat16):
    drawn = jax.random.normal(own_key, dims, jnp.float32) * width
    if len(cuts) > 0:
        drawn = block_levels(own_key, dims, cuts, -0.22, 0.18) * drawn
    return jnp.clip(drawn, min=-reach, max=reach).astype(kind)


def setup_inputs(seed: int = 0) -> dict:
    key_of = jax.random.split(jax.random.key(seed), 9)
    return {
        "tokens": scatter_about(key_of[0], (LEV, NLAT, NLON, D), 1.0, 6.0, ((1, 8), (2, 16))),
        "region_ids": draw_region_ids(jax.random.fold_in(key_of[8], 71), 0),
        "w_qkv": draw_w_qkv(jax.random.fold_in(key_of[8], 71), 0),
        "w_proj": scatter_about(key_of[3], (2, D, D), D ** -0.5, 0.25),
        "w_up": scatter_about(key_of[4], (2, D, FF), D ** -0.5, 0.25),
        "w_down": scatter_about(key_of[5], (2, FF, D), FF ** -0.5, 0.125),
        "merge_first": scatter_about(key_of[6], (4 * D, 2 * D), (4 * D) ** -0.5, 0.125),
        "merge_second": scatter_about(key_of[7], (8 * D, 4 * D), (8 * D) ** -0.5, 0.09375, ((1, 16),)),
    }


EPS = 1e-05

def layer_norm(values):
    values = values.astype(jnp.float32)
    center = values - lax.optimization_barrier(jnp.mean(values, axis=-1, keepdims=True))
    spread = lax.optimization_barrier(jnp.mean(center * center, axis=-1, keepdims=True))
    return center * lax.rsqrt(spread + EPS)

def big_dot(form, left, right):
    return jnp.einsum(form, left.astype(jnp.float32), right.astype(jnp.float32), precision=lax.Precision.HIGHEST)

def to_windows(field_in):
    level_count, row_count, col_count, feature_dim = field_in.shape
    pieces = field_in.reshape(level_count, row_count // WIN_LAT, WIN_LAT, col_count // WIN_LON, WIN_LON, feature_dim)
    pieces = pieces.transpose(1, 3, 0, 2, 4, 5)
    return pieces.reshape(-1, level_count * WIN_LAT * WIN_LON, feature_dim)

def from_windows(pieces, level_count, row_count, col_count):
    feature_dim = pieces.shape[-1]
    field_out = pieces.reshape(row_count // WIN_LAT, col_count // WIN_LON, level_count, WIN_LAT, WIN_LON, feature_dim)
    return field_out.transpose(2, 0, 3, 1, 4, 5).reshape(level_count, row_count, col_count, feature_dim)

def id_windows(region_map, level_count):
    row_count, col_count = region_map.shape
    pieces = region_map.reshape(row_count // WIN_LAT, WIN_LAT, col_count // WIN_LON, WIN_LON).transpose(0, 2, 1, 3)
    pieces = pieces.reshape(-1, WIN_LAT * WIN_LON)
    return jnp.tile(pieces, (1, level_count))

def attend(field_in, window_ids, w_qkv, w_proj):
    level_count, row_count, col_count, feature_dim = field_in.shape
    head_width = feature_dim // HEADS
    windows = to_windows(field_in)
    normed = layer_norm(windows).astype(jnp.bfloat16)
    projections = big_dot('wsd,de->wse', normed, w_qkv).astype(jnp.bfloat16)
    window_count, window_len = (projections.shape[0], projections.shape[1])
    projections = projections.reshape(window_count, window_len, 3, HEADS, head_width)
    scores = big_dot('wqhc,wkhc->whqk', projections[:, :, 0], projections[:, :, 1]) * head_width ** (-0.5)
    if window_ids is not None:
        same_region = window_ids[:, :, None] == window_ids[:, None, :]
        scores = jnp.where(same_region[:, None], scores, -1e+30)
    row_max = lax.optimization_barrier(jnp.max(scores, axis=-1, keepdims=True))
    probs = jnp.exp(scores - row_max)
    probs = (probs / lax.optimization_barrier(jnp.sum(probs, axis=-1, keepdims=True))).astype(jnp.bfloat16)
    blended = big_dot('whqk,wkhc->wqhc', probs, projections[:, :, 2]).astype(jnp.bfloat16)
    blended = blended.reshape(window_count, window_len, feature_dim)
    summed = (windows.astype(jnp.float32) + big_dot('wsd,de->wse', blended, w_proj)).astype(jnp.bfloat16)
    return from_windows(summed, level_count, row_count, col_count)

def feed_forward(field_in, w_up, w_down):
    normed = layer_norm(field_in).astype(jnp.bfloat16)
    hidden = jax.nn.gelu(big_dot('lrcd,df->lrcf', normed, w_up), approximate=False).astype(jnp.bfloat16)
    return (field_in.astype(jnp.float32) + big_dot('lrcf,fd->lrcd', hidden, w_down)).astype(jnp.bfloat16)

def apply_block(field_in, region_map, w_qkv, w_proj, w_up, w_down, masked):
    level_count, row_count, col_count, feature_dim = field_in.shape
    bands = field_in.reshape(level_count, row_count // WIN_LAT, WIN_LAT, col_count, feature_dim).transpose(1, 0, 2, 3, 4)
    id_bands = region_map.reshape(row_count // WIN_LAT, WIN_LAT, col_count)

    def one_band(pair):
        band, band_ids = pair
        window_ids = id_windows(band_ids, level_count) if masked else None
        return feed_forward(attend(band, window_ids, w_qkv, w_proj), w_up, w_down)
    out_bands = lax.map(one_band, (bands, id_bands))
    return out_bands.transpose(1, 0, 2, 3, 4).reshape(level_count, row_count, col_count, feature_dim)

def merge_normed(field_in):
    quads = (field_in[:, 0::2, 0::2], field_in[:, 1::2, 0::2], field_in[:, 0::2, 1::2], field_in[:, 1::2, 1::2])
    return layer_norm(jnp.concatenate(quads, axis=-1)).astype(jnp.bfloat16)

def reference(tokens, region_ids, w_qkv, w_proj, w_up, w_down, merge_first, merge_second):
    first = apply_block(tokens, region_ids, w_qkv[0], w_proj[0], w_up[0], w_down[0], False)
    rolled = jnp.roll(first, (-SHIFT_LAT, -SHIFT_LON), axis=(1, 2))
    rolled_ids = jnp.roll(region_ids, (-SHIFT_LAT, -SHIFT_LON), axis=(0, 1))
    second = apply_block(rolled, rolled_ids, w_qkv[1], w_proj[1], w_up[1], w_down[1], True)
    fine = jnp.roll(second, (SHIFT_LAT, SHIFT_LON), axis=(1, 2))
    merged = big_dot('lrcd,de->lrce', merge_normed(fine), merge_first).astype(jnp.bfloat16)
    coarse = big_dot('lrcd,de->lrce', merge_normed(merged), merge_second).astype(jnp.bfloat16)
    return (fine, coarse)
```

```python
import functools

import jax
import jax.numpy as jnp
import numpy as np
from jax import lax
from jax.experimental import pallas as pl
from jax.experimental.pallas import tpu as pltpu
from jax.sharding import PartitionSpec as P

MESH = pl.DeviceIdType.MESH
BF = jnp.bfloat16
F32 = jnp.float32
EPS = 1e-05
D = 512
FF = 2048
CELL = 64
WIN = 4 * CELL
SCORE_SCALE = 0.125 * 1.4426950408889634
NEG = -1e30

ERF_P = 0.3275911 * 0.7071067811865476
ERF_A = tuple(0.5 * a for a in (0.254829592, -0.284496736, 1.421413741, -1.453152027, 1.061405429))


def tables():
    out_of = np.zeros((432, 512), np.float32)
    for level in range(3):
        for row in range(6):
            for col in range(24):
                cell = (row // 3) * 4 + col // 6
                within = level * 18 + (row % 3) * 6 + col % 6
                out_of[level * 144 + row * 24 + col, cell * CELL + within] = 1
    quads = np.zeros((4 * 256, 16 * CELL), np.float32)
    for q1 in range(4):
        for q2 in range(4):
            for level in range(3):
                for i2 in range(3):
                    for j2 in range(6):
                        i, j = 2 * i2 + q2 % 2, 2 * j2 + q2 // 2
                        row, col = 2 * i + q1 % 2, 2 * j + q1 // 2
                        cell = (row // 3) * 4 + col // 6
                        within = level * 18 + (row % 3) * 6 + col % 6
                        quads[q1 * 256 + q2 * 64 + level * 18 + i2 * 6 + j2, cell * CELL + within] = 1
    place = np.zeros((4 * WIN, 256), np.float32)
    for w in range(4):
        for cell in range(4):
            for within in range(CELL):
                t = w * WIN + cell * CELL + within
                if within >= 54:
                    place[t, 15] = 1
                    place[t, 128] = 1
                else:
                    row = 6 * (w // 2) + 3 * (cell // 2) + (within // 6) % 3
                    col = 12 * (w % 2) + 6 * (cell % 2) + within % 6
                    place[t, row] = 1
                    place[t, 128 + col] = 1
    return out_of, quads, place


def dot(a, b):
    return jnp.dot(a, b, preferred_element_type=F32)


def dot_nt(a, b):
    return lax.dot_general(a, b, (((1,), (1,)), ((), ())), preferred_element_type=F32)


def layer_norm(v):
    center = v - jnp.mean(v, axis=-1, keepdims=True)
    spread = jnp.mean(center * center, axis=-1, keepdims=True)
    return center * lax.rsqrt(spread + EPS)


def gelu(u):
    size = jnp.abs(u)
    t = pl.reciprocal(1.0 + ERF_P * size, approx=True)
    a1, a2, a3, a4, a5 = ERF_A
    poly = t * (a1 + t * (a2 + t * (a3 + t * (a4 + t * a5))))
    tail = size * (poly * jnp.exp2(u * u * (-0.5 * 1.4426950408889634)))
    return jnp.maximum(u, 0.0) - tail


def window_block(cells, r, c, l, bias, b, wqkv, wproj, wup, wdown, qkv, att, mid, acc):
    x = cells[pl.ds(r, 2), pl.ds(c, 2)].reshape(WIN, D).astype(F32)
    normed = layer_norm(x).astype(BF)
    for k in range(3):
        cols = slice(k * 512, (k + 1) * 512)
        qkv[:, cols] = dot(normed, wqkv[l, :, cols]).astype(BF)
    low = lax.broadcasted_iota(jnp.int32, (WIN, 128), 1) < 64
    ones = jnp.ones((WIN, 128), BF)
    zero = jnp.zeros((WIN, 128), BF)
    for pair in range(4):
        q = qkv[:, pair * 128 : (pair + 1) * 128]
        k = qkv[:, 512 + pair * 128 : 512 + (pair + 1) * 128]
        v = jnp.concatenate([qkv[:, 1024 + pair * 128 : 1024 + (pair + 1) * 128], ones], axis=1)
        outs = []
        for part in range(2):
            qm = jnp.where(low, q, zero) if part == 0 else jnp.where(low, zero, q)
            s = dot_nt(qm, k) + bias[b]
            m = jnp.max(s, axis=-1, keepdims=True)
            p = jnp.exp2((s - m) * SCORE_SCALE).astype(BF)
            o = dot(p, v)
            outs.append(o[:, :128] * pl.reciprocal(o[:, 128:], approx=False))
        att[:, pair * 128 : (pair + 1) * 128] = jnp.where(low, outs[0], outs[1]).astype(BF)
    middle = (x + dot(att[...], wproj[l])).astype(BF).astype(F32)
    acc[...] = middle
    mid[...] = layer_norm(middle).astype(BF)
    for k in range(4):
        cols = slice(k * 512, (k + 1) * 512)
        hidden = gelu(dot(mid[...], wup[l, :, cols])).astype(BF)
        acc[...] += dot(hidden, wdown[l, cols, :])
    cells[pl.ds(r, 2), pl.ds(c, 2)] = acc[...].astype(BF).reshape(2, 2, CELL, D)


def kernel(
    tok_h, ids_h, wqkv_h, wproj_h, wup_h, wdown_h, wm1_h, wm2_h, pin_h, pout_h, quads_h, place_h,
    fine_o, coarse_o,
    tok, ids, wqkv, wproj, wup, wdown, wm1, w2, pin, pout, quads, place,
    cells, ret, bias, qkv, att, mid, acc, nq, rows, cown, cgive, cret, fine_s, coarse_s,
    lsem, osem, hsend, hrecv, wsend, wrecv,
):
    lat, lon = lax.axis_index("lat"), lax.axis_index("lon")
    xh, xl = lax.div(lat, 4), lax.div(lon, 8)
    z, core = lax.rem(lax.div(lon, 2), 4), lax.rem(lon, 2)
    lat_up, lat_dn = lax.rem(lat + 1, 8), lax.rem(lat + 7, 8)
    lon_up, lon_dn = lax.rem(lon + 1, 16), lax.rem(lon + 15, 16)
    z_up, z_dn, z_far = lax.rem(z + 1, 4), lax.rem(z + 3, 4), lax.rem(z + 2, 4)
    above, below = (lat, xl * 8 + z_up * 2 + core), (lat, xl * 8 + z_dn * 2 + core)
    side_a = (lat, (1 - xl) * 8 + z * 2 + core)
    side_b = (lax.rem(lat + 4, 8), (1 - xl) * 8 + z * 2 + core)
    twin = (lat, xl * 8 + z * 2 + 1 - core)
    partners = (
        (lat_up, lon), (lat_dn, lon), (lat, lon_up), (lat, lon_dn), (lat_up, lon_up), (lat_dn, lon_dn),
        above, below, side_a, side_b, twin,
    )
    barrier = pltpu.get_barrier_semaphore()
    for device in partners:
        pl.semaphore_signal(barrier, inc=1, device_id=device, device_id_type=MESH)

    mine = xl * 4 + z
    loads = [
        (tok_h, tok), (pin_h, pin), (ids_h, ids), (place_h, place),
        (wqkv_h.at[0], wqkv.at[0]), (wproj_h.at[0], wproj.at[0]), (wup_h.at[0], wup.at[0]), (wdown_h.at[0], wdown.at[0]),
        (wqkv_h.at[1], wqkv.at[1]), (wproj_h.at[1], wproj.at[1]), (wup_h.at[1], wup.at[1]), (wdown_h.at[1], wdown.at[1]),
        (pout_h, pout), (quads_h, quads), (wm1_h, wm1), (wm2_h, w2.at[mine]),
    ]
    loads = [pltpu.make_async_copy(src, dst, lsem.at[i]) for i, (src, dst) in enumerate(loads)]
    for load in loads:
        load.start()

    def halo(i, src, dst, device):
        return pltpu.make_async_remote_copy(
            src_ref=src, dst_ref=dst, send_sem=hsend.at[i], recv_sem=hrecv.at[i], device_id=device, device_id_type=MESH
        )

    def give(i, src, dst, device):
        return pltpu.make_async_remote_copy(
            src_ref=src, dst_ref=dst, send_sem=wsend.at[i], recv_sem=wrecv.at[i], device_id=device, device_id_type=MESH
        )

    half = (pl.ds(0, 2048), pl.ds(2048, 2048))
    s_dn, s_up, s_far = xl * 4 + z_dn, xl * 4 + z_up, xl * 4 + z_far
    weights = [
        give(0, wm2_h, w2.at[mine], above),
        give(1, wm2_h, w2.at[mine], below),
        give(2, wm2_h.at[half[0]], w2.at[mine, half[0]], side_a),
        give(3, wm2_h.at[half[1]], w2.at[mine, half[1]], side_b),
        give(4, w2.at[s_dn, half[0]], w2.at[s_dn, half[0]], above),
        give(5, w2.at[s_up, half[1]], w2.at[s_up, half[1]], below),
        give(6, w2.at[s_dn, half[0]], w2.at[s_dn, half[0]], side_a),
        give(7, w2.at[s_dn, half[1]], w2.at[s_dn, half[1]], side_b),
        give(8, w2.at[s_up, half[0]], w2.at[s_up, half[0]], side_a),
        give(9, w2.at[s_up, half[1]], w2.at[s_up, half[1]], side_b),
        give(10, w2.at[s_far, half[0]], w2.at[s_far, half[0]], side_a),
        give(11, w2.at[s_far, half[1]], w2.at[s_far, half[1]], side_b),
        give(12, rows.at[0], rows.at[1], twin),
        give(13, cgive, cret, twin),
    ]
    out1 = [
        halo(0, cells.at[0, 0], cells.at[4, 4], (lat_dn, lon_dn)),
        halo(1, cells.at[0, 1], cells.at[4, 1], (lat_dn, lon)),
        halo(2, cells.at[1, 0], cells.at[1, 4], (lat, lon_dn)),
        halo(3, cells.at[0, pl.ds(2, 2)], cells.at[4, pl.ds(2, 2)], (lat_dn, lon)),
        halo(4, cells.at[pl.ds(2, 2), 0], cells.at[pl.ds(2, 2), 4], (lat, lon_dn)),
    ]
    out2 = [
        halo(5, cells.at[4, 4], ret.at[0], (lat_up, lon_up)),
        halo(6, cells.at[4, 3], ret.at[3], (lat_up, lon)),
        halo(7, cells.at[3, 4], ret.at[6], (lat, lon_up)),
        halo(8, cells.at[pl.ds(1, 2), 4], ret.at[pl.ds(4, 2)], (lat, lon_up)),
        halo(9, cells.at[4, pl.ds(1, 2)], ret.at[pl.ds(1, 2)], (lat_up, lon)),
    ]

    loads[0].wait()
    loads[1].wait()
    for pair in range(2):
        x = jnp.concatenate([tok[level * 288 + pair * 144 : level * 288 + (pair + 1) * 144, :] for level in range(3)], axis=0)
        y = dot(pin[...], x).astype(BF).reshape(2, 4, CELL, D)
        cells[2 * pair : 2 * pair + 2, 0:4] = y

    pl.semaphore_wait(barrier, len(partners))
    for k in range(4):
        weights[k].start()

    loads[2].wait()
    loads[3].wait()
    at = lax.broadcasted_iota(jnp.int32, (16, 96), 1) - lax.broadcasted_iota(jnp.int32, (16, 96), 0) - (lat * 12 + 3)
    rel = lax.broadcasted_iota(jnp.int32, (16, 96), 0)
    pick_row = jnp.where(((at == 0) | (at == -96)) & (rel < 12), 1.0, 0.0).astype(BF)
    at = lax.broadcasted_iota(jnp.int32, (384, 128), 0) - lax.broadcasted_iota(jnp.int32, (384, 128), 1) - (lon * 24 + 6)
    pick_col = jnp.where((at == 0) | (at == -384), 1.0, 0.0).astype(BF)
    near = dot(dot(pick_row, ids[...].astype(F32).astype(BF)).astype(BF), pick_col)
    near = jnp.where(lax.broadcasted_iota(jnp.int32, (16, 128), 0) == 15, -1.0, near).astype(BF)
    for w in range(4):
        spread = dot(place[w * WIN : (w + 1) * WIN, 0:16], near) * place[w * WIN : (w + 1) * WIN, 128:256].astype(F32)
        column = jnp.sum(spread, axis=1, keepdims=True)
        line = dot_nt(jnp.ones((8, 128), BF), spread.astype(BF))[0:1, :]
        if w == 0:
            bias[0] = jnp.broadcast_to(jnp.where(line < -0.5, NEG, 0.0), (WIN, WIN))
        bias[w + 1] = jnp.where(column == line, 0.0, NEG)

    def step(t, carry):
        @pl.when(t == 0)
        def _():
            for k in range(4, 8):
                loads[k].wait()

        @pl.when(t == 1)
        def _():
            out1[0].start()
            out1[1].start()
            out1[2].start()

        @pl.when(t == 2)
        def _():
            out1[3].start()

        @pl.when(t == 3)
        def _():
            out1[4].start()

        @pl.when(t == 4)
        def _():
            for k in range(8, 12):
                loads[k].wait()
            for k in range(5):
                out1[k].wait()
            weights[0].wait_recv()
            weights[1].wait_recv()
            for k in range(4, 10):
                weights[k].start()

        @pl.when(t == 5)
        def _():
            out2[0].start()
            out2[1].start()
            out2[2].start()

        @pl.when(t == 6)
        def _():
            out2[3].start()

        @pl.when(t == 7)
        def _():
            out2[4].start()
            weights[4].wait_recv()
            weights[5].wait_recv()
            weights[10].start()
            weights[11].start()

        l = t // 4
        u = t - 4 * l
        wr = 1 - u % 2
        wc = 1 - u // 2
        r = l * (1 + 2 * wr) + (1 - l) * 2 * (u // 2)
        c = l * (1 + 2 * wc) + (1 - l) * 2 * (u % 2)
        b = l * (1 + 2 * wr + wc)
        window_block(cells, r, c, l, bias, b, wqkv, wproj, wup, wdown, qkv, att, mid, acc)
        return carry

    lax.fori_loop(0, 8, step, 0)

    for k in range(5):
        out2[k].wait()
    for k in range(4):
        cells[0, k] = ret[k]
    for k in range(3):
        cells[k + 1, 0] = ret[k + 4]

    for k in range(12, 15):
        loads[k].wait()
    for pair in range(2):
        v = dot(pout[...], cells[2 * pair : 2 * pair + 2, 0:4].reshape(8 * CELL, D)).astype(BF)
        for level in range(3):
            fine_s[level * 288 + pair * 144 : level * 288 + (pair + 1) * 144, :] = v[level * 144 : (level + 1) * 144]
    fine_copy = pltpu.make_async_copy(fine_s, fine_o, osem.at[0])
    fine_copy.start()

    every = cells[0:4, 0:4].reshape(16 * CELL, D)
    quad = [dot(quads[k * 256 : (k + 1) * 256, :], every) for k in range(4)]
    normed = layer_norm(jnp.concatenate(quad, axis=1)).astype(BF)
    nq[...] = normed
    merged = dot(nq[...], wm1[...]).astype(BF).astype(F32)
    second = layer_norm(jnp.concatenate([merged[k * 64 : (k + 1) * 64] for k in range(4)], axis=1)).astype(BF)
    rows[0] = second
    weights[12].start()

    loads[15].wait()
    for k in (2, 3, 6, 7, 8, 9, 10, 11):
        weights[k].wait_recv()
    weights[12].wait()

    def columns(j, carry):
        left = jnp.concatenate([rows[0], rows[1]], axis=0)
        right = jnp.concatenate([w2[2 * j], w2[2 * j + 1]], axis=1)
        res = dot(left, right).astype(BF)
        cown[2 * j] = res[0:64, 0:128]
        cown[2 * j + 1] = res[0:64, 128:256]
        cgive[2 * j] = res[64:128, 0:128]
        cgive[2 * j + 1] = res[64:128, 128:256]
        return carry

    lax.fori_loop(0, 4, columns, 0)
    weights[13].start()
    for k in range(8):
        coarse_s[:, pl.ds(pl.multiple_of((2 * k + core) * 128, 128), 128)] = cown[k]
    for k in range(12):
        weights[k].wait_send()
    weights[13].wait()
    for k in range(8):
        coarse_s[:, pl.ds(pl.multiple_of((2 * k + 1 - core) * 128, 128), 128)] = cret[k]
    coarse_copy = pltpu.make_async_copy(coarse_s, coarse_o, osem.at[1])
    coarse_copy.start()
    coarse_copy.wait()
    fine_copy.wait()


def shards(tokens, region_ids, w_qkv, w_proj, w_up, w_down, merge_first, merge_second):
    out_of, quads, place = tables()
    out_of, quads, place = (jnp.asarray(a, BF) for a in (out_of, quads, place))
    vmem = pltpu.VMEM
    fine, coarse = pl.pallas_call(
        kernel,
        out_shape=(jax.ShapeDtypeStruct((864, D), BF), jax.ShapeDtypeStruct((64, 2048), BF)),
        in_specs=[pl.BlockSpec(memory_space=pl.ANY)] * 12,
        out_specs=(pl.BlockSpec(memory_space=pl.ANY),) * 2,
        scratch_shapes=[
            vmem((864, D), BF), vmem((96, 384), jnp.int32), vmem((2, D, 3 * D), BF), vmem((2, D, D), BF),
            vmem((2, D, FF), BF), vmem((2, FF, D), BF), vmem((4 * D, 2 * D), BF), vmem((8, 4096, 128), BF),
            vmem((512, 432), BF), vmem((432, 512), BF), vmem((1024, 1024), BF), vmem((1024, 256), BF),
            vmem((5, 5, CELL, D), BF), vmem((7, CELL, D), BF), vmem((5, WIN, WIN), F32),
            vmem((WIN, 3 * D), BF), vmem((WIN, D), BF), vmem((WIN, D), BF), vmem((WIN, D), F32), vmem((256, 2048), BF),
            vmem((2, 64, 4096), BF), vmem((8, 64, 128), BF), vmem((8, 64, 128), BF), vmem((8, 64, 128), BF),
            vmem((864, D), BF), vmem((64, 2048), BF),
            pltpu.SemaphoreType.DMA((16,)), pltpu.SemaphoreType.DMA((2,)),
            pltpu.SemaphoreType.DMA((10,)), pltpu.SemaphoreType.DMA((10,)),
            pltpu.SemaphoreType.DMA((14,)), pltpu.SemaphoreType.DMA((14,)),
        ],
        compiler_params=pltpu.CompilerParams(
            collective_id=0, has_side_effects=True, vmem_limit_bytes=60 * 1024 * 1024
        ),
    )(
        tokens.reshape(864, D), region_ids, w_qkv, w_proj, w_up, w_down, merge_first, merge_second,
        out_of.T, out_of, quads, place,
    )
    return fine.reshape(3, 12, 24, D), coarse[:54].reshape(3, 3, 6, 2048)


def solution(mesh):
    in_specs = (P(None, "lat", "lon", None), P(), P(), P(), P(), P(), P(), P(None, "lon"))
    out_specs = (P(None, "lat", "lon", None), P(None, "lat", "lon", None))
    return jax.shard_map(shards, mesh=mesh, in_specs=in_specs, out_specs=out_specs, check_vma=False)
```

```python
import functools

import jax
import jax.numpy as jnp
import numpy as np
from jax import lax
from jax.experimental import pallas as pl
from jax.experimental.pallas import tpu as pltpu
from jax.sharding import PartitionSpec as P

MESH = pl.DeviceIdType.MESH
BF = jnp.bfloat16
F32 = jnp.float32
EPS = 1e-05
D = 512
FF = 2048
CELL = 64
WIN = 4 * CELL
SCORE_SCALE = 0.125 * 1.4426950408889634
NEG = -1e30

ERF_T = (0.7978281362947702, 0.03646878884975751, -0.00012486010173499664, -3.058133015679481e-05, 1.1191017522607985e-06)


def tables():
    out_of = np.zeros((432, 512), np.float32)
    for level in range(3):
        for row in range(6):
            for col in range(24):
                cell = (row // 3) * 4 + col // 6
                within = level * 18 + (row % 3) * 6 + col % 6
                out_of[level * 144 + row * 24 + col, cell * CELL + within] = 1
    quads = np.zeros((4 * 256, 16 * CELL), np.float32)
    for q1 in range(4):
        for q2 in range(4):
            for level in range(3):
                for i2 in range(3):
                    for j2 in range(6):
                        i, j = 2 * i2 + q2 % 2, 2 * j2 + q2 // 2
                        row, col = 2 * i + q1 % 2, 2 * j + q1 // 2
                        cell = (row // 3) * 4 + col // 6
                        within = level * 18 + (row % 3) * 6 + col % 6
                        quads[q1 * 256 + q2 * 64 + level * 18 + i2 * 6 + j2, cell * CELL + within] = 1
    place = np.zeros((4 * WIN, 256), np.float32)
    for w in range(4):
        for cell in range(4):
            for within in range(CELL):
                t = w * WIN + cell * CELL + within
                if within >= 54:
                    place[t, 15] = 1
                    place[t, 128] = 1
                else:
                    row = 6 * (w // 2) + 3 * (cell // 2) + (within // 6) % 3
                    col = 12 * (w % 2) + 6 * (cell % 2) + within % 6
                    place[t, row] = 1
                    place[t, 128 + col] = 1
    return out_of, quads, place


def dot(a, b):
    return jnp.dot(a, b, preferred_element_type=F32)


def dot_nt(a, b):
    return lax.dot_general(a, b, (((1,), (1,)), ((), ())), preferred_element_type=F32)


def layer_norm(v):
    center = v - jnp.mean(v, axis=-1, keepdims=True)
    spread = jnp.mean(center * center, axis=-1, keepdims=True)
    return center * lax.rsqrt(spread + EPS)


def gelu(u):
    a = ERF_T
    w = u * u
    h = 0.5 * u
    return h + h * jnp.tanh(u * (a[0] + w * (a[1] + w * (a[2] + w * (a[3] + w * a[4])))))


def window_block(cells, r, c, l, bias, b, wqkv, wproj, wup, wdown, qkv, att, mid, acc, nq, between):
    x = cells[pl.ds(r, 2), pl.ds(c, 2)].reshape(WIN, D).astype(F32)
    normed = layer_norm(x).astype(BF)
    for k in range(3):
        cols = slice(k * 512, (k + 1) * 512)
        qkv[:, cols] = dot(normed, wqkv[l, :, cols]).astype(BF)
    low = lax.broadcasted_iota(jnp.int32, (WIN, 128), 1) < 64
    ones = jnp.ones((WIN, 128), BF)
    zero = jnp.zeros((WIN, 128), BF)
    for pair in range(4):
        q = qkv[:, pair * 128 : (pair + 1) * 128]
        k = qkv[:, 512 + pair * 128 : 512 + (pair + 1) * 128]
        v = jnp.concatenate([qkv[:, 1024 + pair * 128 : 1024 + (pair + 1) * 128], ones], axis=1)
        outs = []
        for part in range(2):
            qm = jnp.where(low, q, zero) if part == 0 else jnp.where(low, zero, q)
            s = dot_nt(qm, k) + bias[b]
            m = jnp.max(s, axis=-1, keepdims=True)
            p = jnp.exp2((s - m) * SCORE_SCALE).astype(BF)
            o = dot(p, v)
            outs.append(o[:, :128] * pl.reciprocal(o[:, 128:], approx=False))
        att[:, pair * 128 : (pair + 1) * 128] = jnp.where(low, outs[0], outs[1]).astype(BF)
    middle = (x + dot(att[...], wproj[l])).astype(BF).astype(F32)
    acc[...] = middle
    mid[...] = layer_norm(middle).astype(BF)
    between()
    nq[...] = gelu(dot(mid[...], wup[l])).astype(BF)
    acc[...] += dot(nq[...], wdown[l])
    cells[pl.ds(r, 2), pl.ds(c, 2)] = acc[...].astype(BF).reshape(2, 2, CELL, D)


def kernel(
    tok_h, ids_h, wqkv_h, wproj_h, wup_h, wdown_h, wm1_h, wm2_h, pin_h, pout_h, quads_h, place_h,
    fine_o, coarse_o,
    tok, ids, wqkv, wproj, wup, wdown, wm1, w2, pin, pout, quads, place,
    cells, ret, bias, qkv, att, mid, acc, nq, rows, cown, cgive, cret, fine_s, flat, coarse_s,
    lsem, osem, hsend, hrecv, wsend, wrecv,
):
    lat, lon = lax.axis_index("lat"), lax.axis_index("lon")
    xh, xl = lax.div(lat, 4), lax.div(lon, 8)
    z, core = lax.rem(lax.div(lon, 2), 4), lax.rem(lon, 2)
    lat_up, lat_dn = lax.rem(lat + 1, 8), lax.rem(lat + 7, 8)
    lon_up, lon_dn = lax.rem(lon + 1, 16), lax.rem(lon + 15, 16)
    z_up, z_dn, z_far = lax.rem(z + 1, 4), lax.rem(z + 3, 4), lax.rem(z + 2, 4)
    above, below = (lat, xl * 8 + z_up * 2 + core), (lat, xl * 8 + z_dn * 2 + core)
    side_a = (lat, (1 - xl) * 8 + z * 2 + core)
    side_b = (lax.rem(lat + 4, 8), (1 - xl) * 8 + z * 2 + core)
    twin = (lat, xl * 8 + z * 2 + 1 - core)
    y = lax.rem(lat, 4)
    p = lax.rem(y, 2)
    next_y = lax.rem(y + 1 + 2 * p, 4)
    other_y = lax.rem(y + 3 - 2 * p, 4)
    pair1, pair2 = (xh * 4 + next_y, lon), (xh * 4 + other_y, lon)
    partners = (
        (lat_up, lon), (lat_dn, lon), (lat, lon_up), (lat, lon_dn), (lat_up, lon_up), (lat_dn, lon_dn),
        above, below, side_a, side_b, twin, pair1, pair2,
    )
    barrier = pltpu.get_barrier_semaphore()
    for device in partners:
        pl.semaphore_signal(barrier, inc=1, device_id=device, device_id_type=MESH)

    mine = xl * 4 + z
    loads = [
        (tok_h, tok), (pin_h, pin), (ids_h, ids), (place_h, place),
        (wqkv_h.at[0], wqkv.at[0]), (wproj_h.at[0], wproj.at[0]), (wup_h.at[0], wup.at[0]), (wdown_h.at[0], wdown.at[0]),
        (wqkv_h.at[1], wqkv.at[1]), (wproj_h.at[1], wproj.at[1]), (wup_h.at[1], wup.at[1]), (wdown_h.at[1], wdown.at[1]),
        (pout_h, pout), (quads_h, quads), (wm1_h, wm1), (wm2_h, w2.at[mine]),
    ]
    loads = [pltpu.make_async_copy(src, dst, lsem.at[i]) for i, (src, dst) in enumerate(loads)]
    for k in range(6):
        loads[k].start()

    def halo(i, src, dst, device):
        return pltpu.make_async_remote_copy(
            src_ref=src, dst_ref=dst, send_sem=hsend.at[i], recv_sem=hrecv.at[i], device_id=device, device_id_type=MESH
        )

    def give(i, src, dst, device):
        return pltpu.make_async_remote_copy(
            src_ref=src, dst_ref=dst, send_sem=wsend.at[i], recv_sem=wrecv.at[i], device_id=device, device_id_type=MESH
        )

    s_dn, s_up, s_far = xl * 4 + z_dn, xl * 4 + z_up, xl * 4 + z_far
    o_dn, o_up, o_far = s_dn + 4 - 8 * xl, s_up + 4 - 8 * xl, s_far + 4 - 8 * xl

    def piece(slot, q, count=1):
        return w2.at[slot, pl.ds(pl.multiple_of(q * 1024, 1024), 1024 * count)]

    def first(q, count=1):
        return wm2_h.at[pl.ds(pl.multiple_of(q * 1024, 1024), 1024 * count)]

    def pass_on(i, slot, q, device):
        return give(i, piece(slot, q), piece(slot, q), device)

    weights = [
        give(0, first(p), piece(mine, p), above),
        give(1, first(1 - p), piece(mine, 1 - p), above),
        give(2, first(2 + p), piece(mine, 2 + p), below),
        give(3, first(3 - p), piece(mine, 3 - p), below),
        give(4, first(0, 2), piece(mine, 0, 2), side_a),
        give(5, first(2, 2), piece(mine, 2, 2), side_b),
        pass_on(6, s_dn, p, above),
        pass_on(7, s_up, 2 + p, below),
        pass_on(8, s_dn, p, side_a),
        pass_on(9, s_up, 2 + p, side_b),
        give(10, first(2), piece(mine, 2), above),
        give(11, first(0), piece(mine, 0), below),
        give(12, first(3), piece(mine, 3), above),
        give(13, first(1), piece(mine, 1), below),
        pass_on(14, s_far, p, side_a),
        pass_on(15, s_far, 2 + p, side_b),
        pass_on(16, s_far, p, pair1),
        pass_on(17, s_far, 2 + p, pair1),
        pass_on(18, o_dn, p, pair2),
        pass_on(19, o_up, 2 + p, pair2),
        pass_on(20, s_up, 0, side_a),
        pass_on(21, s_dn, 2, side_b),
        pass_on(22, s_up, 1, side_a),
        pass_on(23, s_dn, 3, side_b),
        pass_on(24, o_far, p, pair1),
        pass_on(25, o_far, 2 + p, pair1),
        give(26, rows.at[0], rows.at[1], twin),
        give(27, cgive, cret, twin),
    ]

    def stage(received, sent):
        for k in received:
            weights[k].wait_recv()
        for k in sent:
            weights[k].start()

    stages = {
        2: ((0, 2), (6, 7, 8, 9)),
        4: ((), (1, 3)),
        6: ((6, 7), (16, 17, 14, 15, 10, 11)),
        8: ((8, 9), (18, 19)),
        9: ((), (12, 13)),
        11: ((10, 11), (20, 21)),
        12: ((14, 15), (24, 25)),
        14: ((12, 13), (22, 23)),
    }
    last = (1, 3, 4, 5, 16, 17, 18, 19, 20, 21, 22, 23, 24, 25)

    out1 = [
        halo(0, cells.at[0, 0], cells.at[4, 4], (lat_dn, lon_dn)),
        halo(1, cells.at[0, 1], cells.at[4, 1], (lat_dn, lon)),
        halo(2, cells.at[1, 0], cells.at[1, 4], (lat, lon_dn)),
        halo(3, cells.at[0, pl.ds(2, 2)], cells.at[4, pl.ds(2, 2)], (lat_dn, lon)),
        halo(4, cells.at[pl.ds(2, 2), 0], cells.at[pl.ds(2, 2), 4], (lat, lon_dn)),
    ]
    out2 = [
        halo(5, cells.at[4, 4], ret.at[0], (lat_up, lon_up)),
        halo(6, cells.at[4, 3], ret.at[3], (lat_up, lon)),
        halo(7, cells.at[3, 4], ret.at[6], (lat, lon_up)),
        halo(8, cells.at[pl.ds(1, 2), 4], ret.at[pl.ds(4, 2)], (lat, lon_up)),
        halo(9, cells.at[4, pl.ds(1, 2)], ret.at[pl.ds(1, 2)], (lat_up, lon)),
    ]

    loads[0].wait()
    loads[1].wait()
    for pair in range(2):
        x = jnp.concatenate([tok[level * 288 + pair * 144 : level * 288 + (pair + 1) * 144, :] for level in range(3)], axis=0)
        y = dot(pin[...], x).astype(BF).reshape(2, 4, CELL, D)
        cells[2 * pair : 2 * pair + 2, 0:4] = y

    for k in range(6, 8):
        loads[k].start()
    pl.semaphore_wait(barrier, len(partners))
    for k in (0, 2, 4, 5):
        weights[k].start()

    loads[2].wait()
    loads[3].wait()
    at = lax.broadcasted_iota(jnp.int32, (16, 96), 1) - lax.broadcasted_iota(jnp.int32, (16, 96), 0) - (lat * 12 + 3)
    rel = lax.broadcasted_iota(jnp.int32, (16, 96), 0)
    pick_row = jnp.where(((at == 0) | (at == -96)) & (rel < 12), 1.0, 0.0).astype(BF)
    at = lax.broadcasted_iota(jnp.int32, (384, 128), 0) - lax.broadcasted_iota(jnp.int32, (384, 128), 1) - (lon * 24 + 6)
    pick_col = jnp.where((at == 0) | (at == -384), 1.0, 0.0).astype(BF)
    near = dot(dot(pick_row, ids[...].astype(F32).astype(BF)).astype(BF), pick_col)
    near = jnp.where(lax.broadcasted_iota(jnp.int32, (16, 128), 0) == 15, -1.0, near).astype(BF)
    for w in range(4):
        spread = dot(place[w * WIN : (w + 1) * WIN, 0:16], near) * place[w * WIN : (w + 1) * WIN, 128:256].astype(F32)
        column = jnp.sum(spread, axis=1, keepdims=True)
        line = dot_nt(jnp.ones((8, 128), BF), spread.astype(BF))[0:1, :]
        if w == 0:
            bias[0] = jnp.broadcast_to(jnp.where(line < -0.5, NEG, 0.0), (WIN, WIN))
        bias[w + 1] = jnp.where(column == line, 0.0, NEG)

    def step(t, carry):
        @pl.when(t == 0)
        def _():
            for k in range(4, 6):
                loads[k].wait()

        @pl.when(t == 1)
        def _():
            for k in range(3):
                out1[k].start()
            for k in range(8, 16):
                loads[k].start()

        @pl.when(t == 2)
        def _():
            out1[4].start()

        @pl.when(t == 3)
        def _():
            out1[3].start()

        @pl.when(t == 4)
        def _():
            for k in range(8, 12):
                loads[k].wait()

        @pl.when(t == 5)
        def _():
            for k in range(5):
                out1[k].wait()

        @pl.when(t == 6)
        def _():
            for k in range(3):
                out2[k].start()

        @pl.when(t == 7)
        def _():
            out2[4].start()

        for at in range(0, 16, 2):
            if at in stages:
                pl.when(t == at // 2)(functools.partial(stage, *stages[at]))

        def between():
            for at in range(1, 16, 2):
                if at in stages:
                    pl.when(t == at // 2)(functools.partial(stage, *stages[at]))

            @pl.when(t == 0)
            def _():
                for k in range(6, 8):
                    loads[k].wait()

        l = t // 4
        u = t - 4 * l
        odd, high, turn = u % 2, u // 2, ((u + 1) // 2) % 2
        r = l * (1 + 2 * turn) + (1 - l) * 2 * odd
        c = l * (1 + 2 * odd) + (1 - l) * 2 * high
        b = l * (1 + 2 * turn + odd)
        window_block(cells, r, c, l, bias, b, wqkv, wproj, wup, wdown, qkv, att, mid, acc, nq, between)
        return carry

    lax.fori_loop(0, 8, step, 0)

    out2[3].start()
    for k in range(5):
        out2[k].wait()
    for k in range(4):
        cells[0, k] = ret[k]
    for k in range(3):
        cells[k + 1, 0] = ret[k + 4]

    for k in range(12, 15):
        loads[k].wait()
    for pair in range(2):
        v = dot(pout[...], cells[2 * pair : 2 * pair + 2, 0:4].reshape(8 * CELL, D)).astype(BF)
        for level in range(3):
            fine_s[level * 288 + pair * 144 : level * 288 + (pair + 1) * 144, :] = v[level * 144 : (level + 1) * 144]
    fine_copy = pltpu.make_async_copy(fine_s, fine_o, osem.at[0])
    fine_copy.start()

    every = cells[0:4, 0:4].reshape(16 * CELL, D)
    quad = [dot(quads[k * 256 : (k + 1) * 256, :], every) for k in range(4)]
    normed = layer_norm(jnp.concatenate(quad, axis=1)).astype(BF)
    nq[...] = normed
    merged = dot(nq[...], wm1[...]).astype(BF).astype(F32)
    second = layer_norm(jnp.concatenate([merged[k * 64 : (k + 1) * 64] for k in range(4)], axis=1)).astype(BF)
    rows[0] = second
    weights[26].start()

    loads[15].wait()
    for k in last:
        weights[k].wait_recv()
    weights[26].wait()

    def columns(j, carry):
        left = jnp.concatenate([rows[0], rows[1]], axis=0)
        right = jnp.concatenate([w2[2 * j], w2[2 * j + 1]], axis=1)
        res = dot(left, right).astype(BF)
        cown[2 * j] = res[0:64, 0:128]
        cown[2 * j + 1] = res[0:64, 128:256]
        cgive[2 * j] = res[64:128, 0:128]
        cgive[2 * j + 1] = res[64:128, 128:256]
        return carry

    lax.fori_loop(0, 4, columns, 0)
    weights[27].start()
    for k in range(8):
        flat[:, pl.ds(pl.multiple_of((2 * k + core) * 128, 128), 128)] = cown[k].astype(F32)
    for k in range(26):
        weights[k].wait_send()
    weights[27].wait()
    for k in range(8):
        flat[:, pl.ds(pl.multiple_of((2 * k + 1 - core) * 128, 128), 128)] = cret[k].astype(F32)
    for k in range(9):
        coarse_s[k // 3, k % 3] = flat[6 * k : 6 * k + 6, :].astype(BF)
    coarse_copy = pltpu.make_async_copy(coarse_s, coarse_o, osem.at[1])
    coarse_copy.start()
    coarse_copy.wait()
    fine_copy.wait()


def shards(tokens, region_ids, w_qkv, w_proj, w_up, w_down, merge_first, merge_second):
    out_of, quads, place = tables()
    out_of, quads, place = (jnp.asarray(a, BF) for a in (out_of, quads, place))
    vmem = pltpu.VMEM
    fine, coarse = pl.pallas_call(
        kernel,
        out_shape=(jax.ShapeDtypeStruct((864, D), BF), jax.ShapeDtypeStruct((3, 3, 6, 2048), BF)),
        in_specs=[pl.BlockSpec(memory_space=pl.ANY)] * 12,
        out_specs=(pl.BlockSpec(memory_space=pl.ANY),) * 2,
        scratch_shapes=[
            vmem((864, D), BF), vmem((96, 384), jnp.int32), vmem((2, D, 3 * D), BF), vmem((2, D, D), BF),
            vmem((2, D, FF), BF), vmem((2, FF, D), BF), vmem((4 * D, 2 * D), BF), vmem((8, 4096, 128), BF),
            vmem((512, 432), BF), vmem((432, 512), BF), vmem((1024, 1024), BF), vmem((1024, 256), BF),
            vmem((5, 5, CELL, D), BF), vmem((7, CELL, D), BF), vmem((5, WIN, WIN), F32),
            vmem((WIN, 3 * D), BF), vmem((WIN, D), BF), vmem((WIN, D), BF), vmem((WIN, D), F32), vmem((256, 2048), BF),
            vmem((2, 64, 4096), BF), vmem((8, 64, 128), BF), vmem((8, 64, 128), BF), vmem((8, 64, 128), BF),
            vmem((864, D), BF), vmem((64, 2048), F32), vmem((3, 3, 6, 2048), BF),
            pltpu.SemaphoreType.DMA((16,)), pltpu.SemaphoreType.DMA((2,)),
            pltpu.SemaphoreType.DMA((10,)), pltpu.SemaphoreType.DMA((10,)),
            pltpu.SemaphoreType.DMA((28,)), pltpu.SemaphoreType.DMA((28,)),
        ],
        compiler_params=pltpu.CompilerParams(
            collective_id=0, has_side_effects=True, vmem_limit_bytes=60 * 1024 * 1024
        ),
    )(
        tokens.reshape(864, D), region_ids, w_qkv, w_proj, w_up, w_down, merge_first, merge_second,
        out_of.T, out_of, quads, place,
    )
    return fine.reshape(3, 12, 24, D), coarse


def solution(mesh):
    in_specs = (P(None, "lat", "lon", None), P(), P(), P(), P(), P(), P(), P(None, "lon"))
    out_specs = (P(None, "lat", "lon", None), P(None, "lat", "lon", None))
    return jax.shard_map(shards, mesh=mesh, in_specs=in_specs, out_specs=out_specs, check_vma=False)
```

```python
import functools

import jax
import jax.numpy as jnp
import numpy as np
from jax import lax
from jax.experimental import pallas as pl
from jax.experimental.pallas import tpu as pltpu
from jax.sharding import PartitionSpec as P

MESH = pl.DeviceIdType.MESH
BF = jnp.bfloat16
F32 = jnp.float32
EPS = 1e-05
D = 512
FF = 2048
CELL = 64
WIN = 4 * CELL
SCORE_SCALE = 0.125 * 1.4426950408889634
NEG = -1e30

ERF_T = (0.7975078650001068, 0.03700566160227986, -0.00035151904076978317)


def tables():
    out_of = np.zeros((432, 512), np.float32)
    for level in range(3):
        for row in range(6):
            for col in range(24):
                cell = (row // 3) * 4 + col // 6
                within = level * 18 + (row % 3) * 6 + col % 6
                out_of[level * 144 + row * 24 + col, cell * CELL + within] = 1
    quads = np.zeros((4 * 256, 16 * CELL), np.float32)
    for q1 in range(4):
        for q2 in range(4):
            for level in range(3):
                for i2 in range(3):
                    for j2 in range(6):
                        i, j = 2 * i2 + q2 % 2, 2 * j2 + q2 // 2
                        row, col = 2 * i + q1 % 2, 2 * j + q1 // 2
                        cell = (row // 3) * 4 + col // 6
                        within = level * 18 + (row % 3) * 6 + col % 6
                        quads[q1 * 256 + q2 * 64 + level * 18 + i2 * 6 + j2, cell * CELL + within] = 1
    place = np.zeros((4 * WIN, 256), np.float32)
    for w in range(4):
        for cell in range(4):
            for within in range(CELL):
                t = w * WIN + cell * CELL + within
                if within >= 54:
                    place[t, 15] = 1
                    place[t, 128] = 1
                else:
                    row = 6 * (w // 2) + 3 * (cell // 2) + (within // 6) % 3
                    col = 12 * (w % 2) + 6 * (cell % 2) + within % 6
                    place[t, row] = 1
                    place[t, 128 + col] = 1
    return out_of, quads, place


def dot(a, b):
    return jnp.dot(a, b, preferred_element_type=F32)


def dot_nt(a, b):
    return lax.dot_general(a, b, (((1,), (1,)), ((), ())), preferred_element_type=F32)


def layer_norm(v):
    center = v - jnp.mean(v, axis=-1, keepdims=True)
    spread = jnp.mean(center * center, axis=-1, keepdims=True)
    return center * lax.rsqrt(spread + EPS)


def gelu(u):
    u = u.astype(BF)
    a0, a1, a2 = (jnp.asarray(v, BF) for v in ERF_T)
    w = jnp.minimum(u * u, jnp.asarray(26.0, BF))
    h = jnp.asarray(0.5, BF) * u
    return h + h * jnp.tanh(u * (a0 + w * (a1 + w * a2)))


def window_block(cells, r, c, l, bias, b, wqkv, wproj, wup, wdown, qkv, att, mid, acc, nq, between):
    x = cells[pl.ds(r, 2), pl.ds(c, 2)].reshape(WIN, D).astype(F32)
    normed = layer_norm(x).astype(BF)
    for k in range(3):
        cols = slice(k * 512, (k + 1) * 512)
        qkv[:, cols] = dot(normed, wqkv[l, :, cols]).astype(BF)
    low = lax.broadcasted_iota(jnp.int32, (WIN, 128), 1) < 64
    ones = jnp.ones((WIN, 128), BF)
    zero = jnp.zeros((WIN, 128), BF)
    for pair in range(4):
        q = qkv[:, pair * 128 : (pair + 1) * 128]
        k = qkv[:, 512 + pair * 128 : 512 + (pair + 1) * 128]
        v = jnp.concatenate([qkv[:, 1024 + pair * 128 : 1024 + (pair + 1) * 128], ones], axis=1)
        outs = []
        for part in range(2):
            qm = jnp.where(low, q, zero) if part == 0 else jnp.where(low, zero, q)
            s = dot_nt(qm, k) + bias[b]
            m = jnp.max(s, axis=-1, keepdims=True)
            p = jnp.exp2((s - m) * SCORE_SCALE).astype(BF)
            o = dot(p, v)
            outs.append(o[:, :128] * pl.reciprocal(o[:, 128:], approx=False))
        att[:, pair * 128 : (pair + 1) * 128] = jnp.where(low, outs[0], outs[1]).astype(BF)
    middle = (x + dot(att[...], wproj[l])).astype(BF).astype(F32)
    acc[...] = middle
    mid[...] = layer_norm(middle).astype(BF)
    between()
    nq[...] = gelu(dot(mid[...], wup[l])).astype(BF)
    acc[...] += dot(nq[...], wdown[l])
    cells[pl.ds(r, 2), pl.ds(c, 2)] = acc[...].astype(BF).reshape(2, 2, CELL, D)


def kernel(
    tok_h, ids_h, wqkv_h, wproj_h, wup_h, wdown_h, wm1_h, wm2_h, pin_h, pout_h, quads_h, place_h,
    fine_o, coarse_o,
    tok, ids, wqkv, wproj, wup, wdown, wm1, w2, pin, pout, quads, place,
    cells, ret, bias, qkv, att, mid, acc, nq, rows, away, cown, cgive, cret, fgive, fret, fine_s, flat, coarse_s,
    lsem, osem, hsend, hrecv, wsend, wrecv,
):
    lat, lon = lax.axis_index("lat"), lax.axis_index("lon")
    xh, xl = lax.div(lat, 4), lax.div(lon, 8)
    z, core = lax.rem(lax.div(lon, 2), 4), lax.rem(lon, 2)
    lat_up, lat_dn = lax.rem(lat + 1, 8), lax.rem(lat + 7, 8)
    lon_up, lon_dn = lax.rem(lon + 1, 16), lax.rem(lon + 15, 16)
    z_up, z_dn, z_far = lax.rem(z + 1, 4), lax.rem(z + 3, 4), lax.rem(z + 2, 4)
    above, below = (lat, xl * 8 + z_up * 2 + core), (lat, xl * 8 + z_dn * 2 + core)
    side_a = (lat, (1 - xl) * 8 + z * 2 + core)
    side_b = (lax.rem(lat + 4, 8), (1 - xl) * 8 + z * 2 + core)
    side_a2 = (lat, (1 - xl) * 8 + z * 2 + 1 - core)
    side_b2 = (lax.rem(lat + 4, 8), (1 - xl) * 8 + z * 2 + 1 - core)
    twin = (lat, xl * 8 + z * 2 + 1 - core)
    y = lax.rem(lat, 4)
    p = lax.rem(y, 2)
    next_y = lax.rem(y + 1 + 2 * p, 4)
    pair = (xh * 4 + next_y, lon)
    partners = (
        (lat_up, lon), (lat_dn, lon), (lat, lon_up), (lat, lon_dn), (lat_up, lon_up), (lat_dn, lon_dn),
        above, below, side_a, side_b, twin, pair, side_a2, side_b2,
    )
    barrier = pltpu.get_barrier_semaphore()
    for device in partners:
        pl.semaphore_signal(barrier, inc=1, device_id=device, device_id_type=MESH)

    loads = [
        (tok_h, tok), (pin_h, pin), (ids_h, ids), (place_h, place),
        (wqkv_h.at[0], wqkv.at[0]), (wproj_h.at[0], wproj.at[0]), (wup_h.at[0], wup.at[0]), (wdown_h.at[0], wdown.at[0]),
        (wqkv_h.at[1], wqkv.at[1]), (wproj_h.at[1], wproj.at[1]), (wup_h.at[1], wup.at[1]), (wdown_h.at[1], wdown.at[1]),
        (pout_h, pout), (quads_h, quads), (wm1_h, wm1), (wm2_h, w2.at[z]),
    ]
    loads = [pltpu.make_async_copy(src, dst, lsem.at[i]) for i, (src, dst) in enumerate(loads)]
    for k in range(6):
        loads[k].start()

    def halo(i, src, dst, device):
        return pltpu.make_async_remote_copy(
            src_ref=src, dst_ref=dst, send_sem=hsend.at[i], recv_sem=hrecv.at[i], device_id=device, device_id_type=MESH
        )

    def give(i, src, dst, device):
        return pltpu.make_async_remote_copy(
            src_ref=src, dst_ref=dst, send_sem=wsend.at[i], recv_sem=wrecv.at[i], device_id=device, device_id_type=MESH
        )

    def piece(slot, q, count=1):
        return w2.at[slot, pl.ds(pl.multiple_of(q * 1024, 1024), 1024 * count)]

    def first(q, count=1):
        return wm2_h.at[pl.ds(pl.multiple_of(q * 1024, 1024), 1024 * count)]

    def pass_on(i, slot, q, device):
        return give(i, piece(slot, q), piece(slot, q), device)

    weights = [
        give(0, first(p), piece(z, p), above),
        give(1, first(1 - p), piece(z, 1 - p), above),
        give(2, first(2 + p), piece(z, 2 + p), below),
        give(3, first(3 - p), piece(z, 3 - p), below),
        pass_on(4, z_dn, p, above),
        pass_on(5, z_up, 2 + p, below),
        pass_on(6, z_far, p, pair),
        pass_on(7, z_far, 2 + p, pair),
        give(8, first(2), piece(z, 2), above),
        give(9, first(0), piece(z, 0), below),
        give(10, first(3), piece(z, 3), above),
        give(11, first(1), piece(z, 1), below),
    ]
    to_twin = give(12, rows.at[0], rows.at[1], twin)
    from_twin = give(13, cgive, cret, twin)
    across = [
        give(14, rows.at[0, pl.ds(0, 32)], away.at[0], side_a),
        give(15, rows.at[0, pl.ds(32, 32)], away.at[1], side_b),
    ]
    around = [give(16 + k, away.at[k], away.at[2 + k], twin) for k in range(2)]
    back = [give(18 + k, fgive.at[k], fret.at[k], device) for k, device in enumerate((side_a, side_b, side_a2, side_b2))]

    def stage(received, sent):
        for k in received:
            weights[k].wait_recv()
        for k in sent:
            weights[k].start()

    stages = {
        3: ((0, 2), (4, 5)),
        5: ((), (1, 3)),
        8: ((4, 5), (6, 7, 8, 9)),
        11: ((), (10, 11)),
    }
    last = (1, 3, 6, 7, 8, 9, 10, 11)

    out1 = [
        halo(0, cells.at[0, 0], cells.at[4, 4], (lat_dn, lon_dn)),
        halo(1, cells.at[0, 1], cells.at[4, 1], (lat_dn, lon)),
        halo(2, cells.at[1, 0], cells.at[1, 4], (lat, lon_dn)),
        halo(3, cells.at[0, pl.ds(2, 2)], cells.at[4, pl.ds(2, 2)], (lat_dn, lon)),
        halo(4, cells.at[pl.ds(2, 2), 0], cells.at[pl.ds(2, 2), 4], (lat, lon_dn)),
    ]
    out2 = [
        halo(5, cells.at[4, 4], ret.at[0], (lat_up, lon_up)),
        halo(6, cells.at[4, 3], ret.at[3], (lat_up, lon)),
        halo(7, cells.at[3, 4], ret.at[6], (lat, lon_up)),
        halo(8, cells.at[pl.ds(1, 2), 4], ret.at[pl.ds(4, 2)], (lat, lon_up)),
        halo(9, cells.at[4, pl.ds(1, 2)], ret.at[pl.ds(1, 2)], (lat_up, lon)),
    ]

    loads[0].wait()
    loads[1].wait()
    for pair in range(2):
        x = jnp.concatenate([tok[level * 288 + pair * 144 : level * 288 + (pair + 1) * 144, :] for level in range(3)], axis=0)
        y = dot(pin[...], x).astype(BF).reshape(2, 4, CELL, D)
        cells[2 * pair : 2 * pair + 2, 0:4] = y

    for k in range(6, 8):
        loads[k].start()
    pl.semaphore_wait(barrier, len(partners))
    for k in (0, 2):
        weights[k].start()

    loads[2].wait()
    loads[3].wait()
    at = lax.broadcasted_iota(jnp.int32, (16, 96), 1) - lax.broadcasted_iota(jnp.int32, (16, 96), 0) - (lat * 12 + 3)
    rel = lax.broadcasted_iota(jnp.int32, (16, 96), 0)
    pick_row = jnp.where(((at == 0) | (at == -96)) & (rel < 12), 1.0, 0.0).astype(BF)
    at = lax.broadcasted_iota(jnp.int32, (384, 128), 0) - lax.broadcasted_iota(jnp.int32, (384, 128), 1) - (lon * 24 + 6)
    pick_col = jnp.where((at == 0) | (at == -384), 1.0, 0.0).astype(BF)
    near = dot(dot(pick_row, ids[...].astype(F32).astype(BF)).astype(BF), pick_col)
    near = jnp.where(lax.broadcasted_iota(jnp.int32, (16, 128), 0) == 15, -1.0, near).astype(BF)
    for w in range(4):
        spread = dot(place[w * WIN : (w + 1) * WIN, 0:16], near) * place[w * WIN : (w + 1) * WIN, 128:256].astype(F32)
        column = jnp.sum(spread, axis=1, keepdims=True)
        line = dot_nt(jnp.ones((8, 128), BF), spread.astype(BF))[0:1, :]
        if w == 0:
            bias[0] = jnp.broadcast_to(jnp.where(line < -0.5, NEG, 0.0), (WIN, WIN))
        bias[w + 1] = jnp.where(column == line, 0.0, NEG)

    def step(t, carry):
        @pl.when(t == 0)
        def _():
            for k in range(4, 6):
                loads[k].wait()

        @pl.when(t == 1)
        def _():
            for k in range(3):
                out1[k].start()
            for k in range(8, 16):
                loads[k].start()

        @pl.when(t == 2)
        def _():
            out1[4].start()

        @pl.when(t == 3)
        def _():
            out1[3].start()

        @pl.when(t == 4)
        def _():
            for k in range(8, 12):
                loads[k].wait()

        @pl.when(t == 5)
        def _():
            for k in range(5):
                out1[k].wait()

        @pl.when(t == 6)
        def _():
            for k in range(3):
                out2[k].start()

        @pl.when(t == 7)
        def _():
            out2[4].start()

        for at in range(0, 16, 2):
            if at in stages:
                pl.when(t == at // 2)(functools.partial(stage, *stages[at]))

        def between():
            for at in range(1, 16, 2):
                if at in stages:
                    pl.when(t == at // 2)(functools.partial(stage, *stages[at]))

            @pl.when(t == 0)
            def _():
                for k in range(6, 8):
                    loads[k].wait()

        l = t // 4
        u = t - 4 * l
        odd, high, turn = u % 2, u // 2, ((u + 1) // 2) % 2
        r = l * (1 + 2 * turn) + (1 - l) * 2 * odd
        c = l * (1 + 2 * odd) + (1 - l) * 2 * high
        b = l * (1 + 2 * turn + odd)
        window_block(cells, r, c, l, bias, b, wqkv, wproj, wup, wdown, qkv, att, mid, acc, nq, between)
        return carry

    lax.fori_loop(0, 8, step, 0)

    out2[3].start()
    for k in range(5):
        out2[k].wait()
    for k in range(4):
        cells[0, k] = ret[k]
    for k in range(3):
        cells[k + 1, 0] = ret[k + 4]

    for k in range(12, 15):
        loads[k].wait()

    every = cells[0:4, 0:4].reshape(16 * CELL, D)
    quad = [dot(quads[k * 256 : (k + 1) * 256, :], every) for k in range(4)]
    normed = layer_norm(jnp.concatenate(quad, axis=1)).astype(BF)
    nq[...] = normed
    merged = dot(nq[...], wm1[...]).astype(BF).astype(F32)
    second = layer_norm(jnp.concatenate([merged[k * 64 : (k + 1) * 64] for k in range(4)], axis=1)).astype(BF)
    rows[0] = second
    across[0].start()
    across[1].start()
    to_twin.start()

    for pair in range(2):
        v = dot(pout[...], cells[2 * pair : 2 * pair + 2, 0:4].reshape(8 * CELL, D)).astype(BF)
        for level in range(3):
            fine_s[level * 288 + pair * 144 : level * 288 + (pair + 1) * 144, :] = v[level * 144 : (level + 1) * 144]
    fine_copy = pltpu.make_async_copy(fine_s, fine_o, osem.at[0])
    fine_copy.start()

    loads[15].wait()
    for k in last:
        weights[k].wait_recv()
    to_twin.wait()

    def near_columns(j, carry):
        left = jnp.concatenate([rows[0], rows[1]], axis=0)
        res = dot(left, jnp.concatenate([w2[2 * j], w2[2 * j + 1]], axis=1)).astype(BF)
        cown[2 * j] = res[0:64, 0:128]
        cown[2 * j + 1] = res[0:64, 128:256]
        cgive[2 * j] = res[64:128, 0:128]
        cgive[2 * j + 1] = res[64:128, 128:256]
        return carry

    lax.fori_loop(0, 2, near_columns, 0)
    from_twin.start()
    for k in range(2):
        across[k].wait_recv()
        around[k].start()
    for k in range(2):
        around[k].wait_recv()

    def far_columns(j, carry):
        left = away[...].reshape(128, 4096)
        res = dot(left, jnp.concatenate([w2[2 * j], w2[2 * j + 1]], axis=1)).astype(BF)
        for k in range(4):
            fgive[k, 2 * j] = res[32 * k : 32 * k + 32, 0:128]
            fgive[k, 2 * j + 1] = res[32 * k : 32 * k + 32, 128:256]
        return carry

    lax.fori_loop(0, 2, far_columns, 0)
    for copy in back:
        copy.start()

    def block(side, k, c):
        return pl.ds(pl.multiple_of((side * 8 + 2 * k + c) * 128, 128), 128)

    for k in range(12):
        weights[k].wait_send()
    for k in range(2):
        across[k].wait_send()
        around[k].wait_send()
    from_twin.wait()
    for k in range(4):
        flat[:, block(xl, k, core)] = cown[k].astype(F32)
        flat[:, block(xl, k, 1 - core)] = cret[k].astype(F32)
    for copy in back:
        copy.wait()
    for k in range(4):
        flat[0:32, block(1 - xl, k, core)] = fret[0, k].astype(F32)
        flat[32:64, block(1 - xl, k, core)] = fret[1, k].astype(F32)
        flat[0:32, block(1 - xl, k, 1 - core)] = fret[2, k].astype(F32)
        flat[32:64, block(1 - xl, k, 1 - core)] = fret[3, k].astype(F32)
    for k in range(9):
        coarse_s[k // 3, k % 3] = flat[6 * k : 6 * k + 6, :].astype(BF)
    coarse_copy = pltpu.make_async_copy(coarse_s, coarse_o, osem.at[1])
    coarse_copy.start()
    coarse_copy.wait()
    fine_copy.wait()


def hand_over(fine_i, coarse_i, fine_o, coarse_o):
    fine_o[...] = fine_i[...]
    coarse_o[...] = coarse_i[...]


def shards(tokens, region_ids, w_qkv, w_proj, w_up, w_down, merge_first, merge_second):
    out_of, quads, place = tables()
    out_of, quads, place = (jnp.asarray(a, BF) for a in (out_of, quads, place))
    vmem = pltpu.VMEM
    fine, coarse = pl.pallas_call(
        kernel,
        out_shape=(jax.ShapeDtypeStruct((864, D), BF), jax.ShapeDtypeStruct((3, 3, 6, 2048), BF)),
        in_specs=[pl.BlockSpec(memory_space=pl.ANY)] * 12,
        out_specs=(pl.BlockSpec(memory_space=pl.ANY),) * 2,
        scratch_shapes=[
            vmem((864, D), BF), vmem((96, 384), jnp.int32), vmem((2, D, 3 * D), BF), vmem((2, D, D), BF),
            vmem((2, D, FF), BF), vmem((2, FF, D), BF), vmem((4 * D, 2 * D), BF), vmem((4, 4096, 128), BF),
            vmem((512, 432), BF), vmem((432, 512), BF), vmem((1024, 1024), BF), vmem((1024, 256), BF),
            vmem((5, 5, CELL, D), BF), vmem((7, CELL, D), BF), vmem((5, WIN, WIN), F32),
            vmem((WIN, 3 * D), BF), vmem((WIN, D), BF), vmem((WIN, D), BF), vmem((WIN, D), F32), vmem((256, 2048), BF),
            vmem((2, 64, 4096), BF), vmem((4, 32, 4096), BF), vmem((4, 64, 128), BF), vmem((4, 64, 128), BF), vmem((4, 64, 128), BF),
            vmem((4, 4, 32, 128), BF), vmem((4, 4, 32, 128), BF),
            vmem((864, D), BF), vmem((64, 2048), F32), vmem((3, 3, 6, 2048), BF),
            pltpu.SemaphoreType.DMA((16,)), pltpu.SemaphoreType.DMA((2,)),
            pltpu.SemaphoreType.DMA((10,)), pltpu.SemaphoreType.DMA((10,)),
            pltpu.SemaphoreType.DMA((22,)), pltpu.SemaphoreType.DMA((22,)),
        ],
        compiler_params=pltpu.CompilerParams(
            collective_id=0, has_side_effects=True, vmem_limit_bytes=60 * 1024 * 1024
        ),
    )(
        tokens.reshape(864, D), region_ids, w_qkv, w_proj, w_up, w_down, merge_first, merge_second,
        out_of.T, out_of, quads, place,
    )
    specs = (pl.BlockSpec((288, D), lambda k: (k, 0)), pl.BlockSpec((1, 3, 6, 2048), lambda k: (k, 0, 0, 0)))
    fine, coarse = pl.pallas_call(
        hand_over,
        grid=(3,),
        out_shape=(jax.ShapeDtypeStruct(fine.shape, BF), jax.ShapeDtypeStruct(coarse.shape, BF)),
        in_specs=list(specs),
        out_specs=specs,
    )(fine, coarse)
    return fine.reshape(3, 12, 24, D), coarse


def solution(mesh):
    in_specs = (P(None, "lat", "lon", None), P(), P(), P(), P(), P(), P(), P(None, "lon"))
    out_specs = (P(None, "lat", "lon", None), P(None, "lat", "lon", None))
    return jax.shard_map(shards, mesh=mesh, in_specs=in_specs, out_specs=out_specs, check_vma=False)
```

```python
import functools

import jax
import jax.numpy as jnp
import numpy as np
from jax import lax
from jax.experimental import pallas as pl
from jax.experimental.pallas import tpu as pltpu
from jax.sharding import PartitionSpec as P

MESH = pl.DeviceIdType.MESH
BF = jnp.bfloat16
F32 = jnp.float32
EPS = 1e-05
D = 512
FF = 2048
CELL = 64
WIN = 4 * CELL
SCORE_SCALE = 0.125 * 1.4426950408889634
NEG = -1e30

ERF_T = (0.7975078650001068, 0.03700566160227986, -0.00035151904076978317)


def tables():
    out_of = np.zeros((432, 512), np.float32)
    for level in range(3):
        for row in range(6):
            for col in range(24):
                cell = (row // 3) * 4 + col // 6
                within = level * 18 + (row % 3) * 6 + col % 6
                out_of[level * 144 + row * 24 + col, cell * CELL + within] = 1
    quads = np.zeros((4 * 256, 16 * CELL), np.float32)
    for q1 in range(4):
        for q2 in range(4):
            for level in range(3):
                for i2 in range(3):
                    for j2 in range(6):
                        i, j = 2 * i2 + q2 % 2, 2 * j2 + q2 // 2
                        row, col = 2 * i + q1 % 2, 2 * j + q1 // 2
                        cell = (row // 3) * 4 + col // 6
                        within = level * 18 + (row % 3) * 6 + col % 6
                        quads[q1 * 256 + q2 * 64 + level * 18 + i2 * 6 + j2, cell * CELL + within] = 1
    place = np.zeros((4 * WIN, 256), np.float32)
    for w in range(4):
        for cell in range(4):
            for within in range(CELL):
                t = w * WIN + cell * CELL + within
                if within >= 54:
                    place[t, 15] = 1
                    place[t, 128] = 1
                else:
                    row = 6 * (w // 2) + 3 * (cell // 2) + (within // 6) % 3
                    col = 12 * (w % 2) + 6 * (cell % 2) + within % 6
                    place[t, row] = 1
                    place[t, 128 + col] = 1
    return out_of, quads, place


def dot(a, b):
    return jnp.dot(a, b, preferred_element_type=F32)


def dot_nt(a, b):
    return lax.dot_general(a, b, (((1,), (1,)), ((), ())), preferred_element_type=F32)


def layer_norm(v):
    center = v - jnp.mean(v, axis=-1, keepdims=True)
    spread = jnp.mean(center * center, axis=-1, keepdims=True)
    return center * lax.rsqrt(spread + EPS)


def gelu(u):
    u = u.astype(BF)
    a0, a1, a2 = (jnp.asarray(v, BF) for v in ERF_T)
    w = jnp.minimum(u * u, jnp.asarray(26.0, BF))
    h = jnp.asarray(0.5, BF) * u
    return h + h * jnp.tanh(u * (a0 + w * (a1 + w * a2)))


def window_block(cells, r, c, l, bias, b, wqkv, wproj, wup, wdown, qkv, att, mid, acc, nq, between):
    x = cells[pl.ds(r, 2), pl.ds(c, 2)].reshape(WIN, D).astype(F32)
    normed = layer_norm(x).astype(BF)
    for k in range(3):
        cols = slice(k * 512, (k + 1) * 512)
        qkv[:, cols] = dot(normed, wqkv[l, :, cols]).astype(BF)
    low = lax.broadcasted_iota(jnp.int32, (WIN, 128), 1) < 64
    ones = jnp.ones((WIN, 128), BF)
    zero = jnp.zeros((WIN, 128), BF)
    for pair in range(4):
        q = qkv[:, pair * 128 : (pair + 1) * 128]
        k = qkv[:, 512 + pair * 128 : 512 + (pair + 1) * 128]
        v = jnp.concatenate([qkv[:, 1024 + pair * 128 : 1024 + (pair + 1) * 128], ones], axis=1)
        outs = []
        for part in range(2):
            qm = jnp.where(low, q, zero) if part == 0 else jnp.where(low, zero, q)
            s = dot_nt(qm, k) + bias[b]
            m = jnp.max(s, axis=-1, keepdims=True)
            p = jnp.exp2((s - m) * SCORE_SCALE).astype(BF)
            o = dot(p, v)
            outs.append(o[:, :128] * pl.reciprocal(o[:, 128:], approx=False))
        att[:, pair * 128 : (pair + 1) * 128] = jnp.where(low, outs[0], outs[1]).astype(BF)
    middle = (x + dot(att[...], wproj[l])).astype(BF).astype(F32)
    acc[...] = middle
    mid[...] = layer_norm(middle).astype(BF)
    between()
    nq[...] = gelu(dot(mid[...], wup[l])).astype(BF)
    acc[...] += dot(nq[...], wdown[l])
    cells[pl.ds(r, 2), pl.ds(c, 2)] = acc[...].astype(BF).reshape(2, 2, CELL, D)


def kernel(
    tok_h, ids_h, wqkv_h, wproj_h, wup_h, wdown_h, wm1_h, wm2_h, pin_h, pout_h, quads_h, place_h,
    fine_o, coarse_o,
    tok, ids, wqkv, wproj, wup, wdown, wm1, w2, pin, pout, quads, place,
    cells, ret, bias, qkv, att, mid, acc, nq, rows, away, cown, cgive, cret, fgive, fret, fine_s, flat, coarse_s,
    lsem, osem, hsend, hrecv, wsend, wrecv,
):
    lat, lon = lax.axis_index("lat"), lax.axis_index("lon")
    xh, xl = lax.div(lat, 4), lax.div(lon, 8)
    z, core = lax.rem(lax.div(lon, 2), 4), lax.rem(lon, 2)
    lat_up, lat_dn = lax.rem(lat + 1, 8), lax.rem(lat + 7, 8)
    lon_up, lon_dn = lax.rem(lon + 1, 16), lax.rem(lon + 15, 16)
    z_up, z_dn, z_far = lax.rem(z + 1, 4), lax.rem(z + 3, 4), lax.rem(z + 2, 4)
    above, below = (lat, xl * 8 + z_up * 2 + core), (lat, xl * 8 + z_dn * 2 + core)
    side_a = (lat, (1 - xl) * 8 + z * 2 + core)
    side_b = (lax.rem(lat + 4, 8), (1 - xl) * 8 + z * 2 + core)
    side_a2 = (lat, (1 - xl) * 8 + z * 2 + 1 - core)
    side_b2 = (lax.rem(lat + 4, 8), (1 - xl) * 8 + z * 2 + 1 - core)
    twin = (lat, xl * 8 + z * 2 + 1 - core)
    y = lax.rem(lat, 4)
    p = lax.rem(y, 2)
    next_y = lax.rem(y + 1 + 2 * p, 4)
    pair = (xh * 4 + next_y, lon)
    partners = (
        (lat_up, lon), (lat_dn, lon), (lat, lon_up), (lat, lon_dn), (lat_up, lon_up), (lat_dn, lon_dn),
        above, below, side_a, side_b, twin, pair, side_a2, side_b2,
    )
    barrier = pltpu.get_barrier_semaphore()
    for device in partners:
        pl.semaphore_signal(barrier, inc=1, device_id=device, device_id_type=MESH)

    loads = [
        (tok_h, tok), (pin_h, pin), (ids_h, ids), (place_h, place),
        (wqkv_h.at[0], wqkv.at[0]), (wproj_h.at[0], wproj.at[0]), (wup_h.at[0], wup.at[0]), (wdown_h.at[0], wdown.at[0]),
        (wqkv_h.at[1], wqkv.at[1]), (wproj_h.at[1], wproj.at[1]), (wup_h.at[1], wup.at[1]), (wdown_h.at[1], wdown.at[1]),
        (pout_h, pout), (quads_h, quads), (wm1_h, wm1), (wm2_h, w2.at[z]),
    ]
    loads = [pltpu.make_async_copy(src, dst, lsem.at[i]) for i, (src, dst) in enumerate(loads)]
    for k in range(6):
        loads[k].start()

    def halo(i, src, dst, device):
        return pltpu.make_async_remote_copy(
            src_ref=src, dst_ref=dst, send_sem=hsend.at[i], recv_sem=hrecv.at[i], device_id=device, device_id_type=MESH
        )

    def give(i, src, dst, device):
        return pltpu.make_async_remote_copy(
            src_ref=src, dst_ref=dst, send_sem=wsend.at[i], recv_sem=wrecv.at[i], device_id=device, device_id_type=MESH
        )

    def piece(slot, q, count=1):
        return w2.at[slot, pl.ds(pl.multiple_of(q * 1024, 1024), 1024 * count)]

    def first(q, count=1):
        return wm2_h.at[pl.ds(pl.multiple_of(q * 1024, 1024), 1024 * count)]

    def pass_on(i, slot, q, device):
        return give(i, piece(slot, q), piece(slot, q), device)

    weights = [
        give(0, first(p), piece(z, p), above),
        give(1, first(1 - p), piece(z, 1 - p), above),
        give(2, first(2 + p), piece(z, 2 + p), below),
        give(3, first(3 - p), piece(z, 3 - p), below),
        pass_on(4, z_dn, p, above),
        pass_on(5, z_up, 2 + p, below),
        pass_on(6, z_far, p, pair),
        pass_on(7, z_far, 2 + p, pair),
        give(8, first(2), piece(z, 2), above),
        give(9, first(0), piece(z, 0), below),
        give(10, first(3), piece(z, 3), above),
        give(11, first(1), piece(z, 1), below),
    ]
    to_twin = give(12, rows.at[0], rows.at[1], twin)
    from_twin = give(13, cgive, cret, twin)
    across = [
        give(14, rows.at[0, pl.ds(0, 16)], away.at[0, pl.ds(0, 16)], side_a),
        give(15, rows.at[0, pl.ds(32, 16)], away.at[1, pl.ds(0, 16)], side_b),
        give(22, rows.at[0, pl.ds(16, 16)], away.at[0, pl.ds(16, 16)], side_a),
        give(23, rows.at[0, pl.ds(48, 16)], away.at[1, pl.ds(16, 16)], side_b),
    ]
    around = [
        give(16, away.at[0, pl.ds(0, 16)], away.at[2, pl.ds(0, 16)], twin),
        give(17, away.at[1, pl.ds(0, 16)], away.at[3, pl.ds(0, 16)], twin),
        give(24, away.at[0, pl.ds(16, 16)], away.at[2, pl.ds(16, 16)], twin),
        give(25, away.at[1, pl.ds(16, 16)], away.at[3, pl.ds(16, 16)], twin),
    ]
    back = [give(18 + k, fgive.at[k], fret.at[k], device) for k, device in enumerate((side_a, side_b, side_a2, side_b2))]

    def stage(received, sent):
        for k in received:
            weights[k].wait_recv()
        for k in sent:
            weights[k].start()

    stages = {
        4: ((0, 2), (4, 5, 1, 3)),
        8: ((4, 5), (6, 7)),
        10: ((), (8, 9, 10, 11)),
    }
    last = (1, 3, 6, 7, 8, 9, 10, 11)

    out1 = [
        halo(0, cells.at[0, 0], cells.at[4, 4], (lat_dn, lon_dn)),
        halo(1, cells.at[0, 1], cells.at[4, 1], (lat_dn, lon)),
        halo(2, cells.at[1, 0], cells.at[1, 4], (lat, lon_dn)),
        halo(3, cells.at[0, pl.ds(2, 2)], cells.at[4, pl.ds(2, 2)], (lat_dn, lon)),
        halo(4, cells.at[pl.ds(2, 2), 0], cells.at[pl.ds(2, 2), 4], (lat, lon_dn)),
    ]
    out2 = [
        halo(5, cells.at[4, 4], ret.at[0], (lat_up, lon_up)),
        halo(6, cells.at[4, 3], ret.at[3], (lat_up, lon)),
        halo(7, cells.at[3, 4], ret.at[6], (lat, lon_up)),
        halo(8, cells.at[pl.ds(1, 2), 4], ret.at[pl.ds(4, 2)], (lat, lon_up)),
        halo(9, cells.at[4, pl.ds(1, 2)], ret.at[pl.ds(1, 2)], (lat_up, lon)),
    ]

    loads[0].wait()
    loads[1].wait()
    for pair in range(2):
        x = jnp.concatenate([tok[level * 288 + pair * 144 : level * 288 + (pair + 1) * 144, :] for level in range(3)], axis=0)
        y = dot(pin[...], x).astype(BF).reshape(2, 4, CELL, D)
        cells[2 * pair : 2 * pair + 2, 0:4] = y

    for k in range(6, 8):
        loads[k].start()
    pl.semaphore_wait(barrier, len(partners))
    for k in (0, 2):
        weights[k].start()

    loads[2].wait()
    loads[3].wait()
    at = lax.broadcasted_iota(jnp.int32, (16, 96), 1) - lax.broadcasted_iota(jnp.int32, (16, 96), 0) - (lat * 12 + 3)
    rel = lax.broadcasted_iota(jnp.int32, (16, 96), 0)
    pick_row = jnp.where(((at == 0) | (at == -96)) & (rel < 12), 1.0, 0.0).astype(BF)
    at = lax.broadcasted_iota(jnp.int32, (384, 128), 0) - lax.broadcasted_iota(jnp.int32, (384, 128), 1) - (lon * 24 + 6)
    pick_col = jnp.where((at == 0) | (at == -384), 1.0, 0.0).astype(BF)
    near = dot(dot(pick_row, ids[...].astype(F32).astype(BF)).astype(BF), pick_col)
    near = jnp.where(lax.broadcasted_iota(jnp.int32, (16, 128), 0) == 15, -1.0, near).astype(BF)
    for w in range(4):
        spread = dot(place[w * WIN : (w + 1) * WIN, 0:16], near) * place[w * WIN : (w + 1) * WIN, 128:256].astype(F32)
        column = jnp.sum(spread, axis=1, keepdims=True)
        line = dot_nt(jnp.ones((8, 128), BF), spread.astype(BF))[0:1, :]
        if w == 0:
            bias[0] = jnp.broadcast_to(jnp.where(line < -0.5, NEG, 0.0), (WIN, WIN))
        bias[w + 1] = jnp.where(column == line, 0.0, NEG)

    def step(t, carry):
        @pl.when(t == 0)
        def _():
            for k in range(4, 6):
                loads[k].wait()

        @pl.when(t == 1)
        def _():
            for k in range(3):
                out1[k].start()
            for k in range(8, 16):
                loads[k].start()

        @pl.when(t == 2)
        def _():
            out1[4].start()

        @pl.when(t == 3)
        def _():
            out1[3].start()

        @pl.when(t == 4)
        def _():
            for k in range(8, 12):
                loads[k].wait()

        @pl.when(t == 5)
        def _():
            for k in range(5):
                out1[k].wait()

        @pl.when(t == 6)
        def _():
            for k in range(3):
                out2[k].start()

        @pl.when(t == 7)
        def _():
            out2[4].start()

        for at in range(0, 16, 2):
            if at in stages:
                pl.when(t == at // 2)(functools.partial(stage, *stages[at]))

        def between():
            for at in range(1, 16, 2):
                if at in stages:
                    pl.when(t == at // 2)(functools.partial(stage, *stages[at]))

            @pl.when(t == 0)
            def _():
                for k in range(6, 8):
                    loads[k].wait()

        l = t // 4
        u = t - 4 * l
        odd, high, turn = u % 2, u // 2, ((u + 1) // 2) % 2
        r = l * (1 + 2 * turn) + (1 - l) * 2 * odd
        c = l * (1 + 2 * odd) + (1 - l) * 2 * high
        b = l * (1 + 2 * turn + odd)
        window_block(cells, r, c, l, bias, b, wqkv, wproj, wup, wdown, qkv, att, mid, acc, nq, between)
        return carry

    lax.fori_loop(0, 8, step, 0)

    out2[3].start()
    for k in range(5):
        out2[k].wait()
    for k in range(4):
        cells[0, k] = ret[k]
    for k in range(3):
        cells[k + 1, 0] = ret[k + 4]

    for k in range(12, 15):
        loads[k].wait()

    every = cells[0:4, 0:4].reshape(16 * CELL, D)
    quad = [dot(quads[k * 256 : (k + 1) * 256, :], every) for k in range(4)]
    normed = layer_norm(jnp.concatenate(quad, axis=1)).astype(BF)
    nq[...] = normed
    merged = dot(nq[...], wm1[...]).astype(BF).astype(F32)
    second = layer_norm(jnp.concatenate([merged[k * 64 : (k + 1) * 64] for k in range(4)], axis=1)).astype(BF)
    rows[0] = second
    to_twin.start()
    for copy in across:
        copy.start()

    for pair in range(2):
        v = dot(pout[...], cells[2 * pair : 2 * pair + 2, 0:4].reshape(8 * CELL, D)).astype(BF)
        for level in range(3):
            fine_s[level * 288 + pair * 144 : level * 288 + (pair + 1) * 144, :] = v[level * 144 : (level + 1) * 144]
    fine_copy = pltpu.make_async_copy(fine_s, fine_o, osem.at[0])
    fine_copy.start()

    loads[15].wait()
    for k in last:
        weights[k].wait_recv()
    to_twin.wait()

    def near_columns(j, carry):
        left = jnp.concatenate([rows[0], rows[1]], axis=0)
        res = dot(left, jnp.concatenate([w2[2 * j], w2[2 * j + 1]], axis=1)).astype(BF)
        cown[2 * j] = res[0:64, 0:128]
        cown[2 * j + 1] = res[0:64, 128:256]
        cgive[2 * j] = res[64:128, 0:128]
        cgive[2 * j + 1] = res[64:128, 128:256]
        return carry

    lax.fori_loop(0, 2, near_columns, 0)
    from_twin.start()
    for k in range(4):
        across[k].wait_recv()
        around[k].start()
    for k in range(4):
        around[k].wait_recv()

    def far_columns(j, carry):
        left = away[...].reshape(128, 4096)
        res = dot(left, jnp.concatenate([w2[2 * j], w2[2 * j + 1]], axis=1)).astype(BF)
        for k in range(4):
            fgive[k, 2 * j] = res[32 * k : 32 * k + 32, 0:128]
            fgive[k, 2 * j + 1] = res[32 * k : 32 * k + 32, 128:256]
        return carry

    lax.fori_loop(0, 2, far_columns, 0)
    for copy in back:
        copy.start()

    def block(side, k, c):
        return pl.ds(pl.multiple_of((side * 8 + 2 * k + c) * 128, 128), 128)

    for k in range(12):
        weights[k].wait_send()
    for k in range(4):
        across[k].wait_send()
        around[k].wait_send()
    from_twin.wait()
    for k in range(4):
        flat[:, block(xl, k, core)] = cown[k].astype(F32)
        flat[:, block(xl, k, 1 - core)] = cret[k].astype(F32)
    for copy in back:
        copy.wait()
    for k in range(4):
        flat[0:32, block(1 - xl, k, core)] = fret[0, k].astype(F32)
        flat[32:64, block(1 - xl, k, core)] = fret[1, k].astype(F32)
        flat[0:32, block(1 - xl, k, 1 - core)] = fret[2, k].astype(F32)
        flat[32:64, block(1 - xl, k, 1 - core)] = fret[3, k].astype(F32)
    for k in range(9):
        coarse_s[k // 3, k % 3] = flat[6 * k : 6 * k + 6, :].astype(BF)
    coarse_copy = pltpu.make_async_copy(coarse_s, coarse_o, osem.at[1])
    coarse_copy.start()
    coarse_copy.wait()
    fine_copy.wait()


def hand_over(fine_i, coarse_i, fine_o, coarse_o):
    fine_o[...] = fine_i[...]
    coarse_o[...] = coarse_i[...]


def shards(tokens, region_ids, w_qkv, w_proj, w_up, w_down, merge_first, merge_second):
    out_of, quads, place = tables()
    out_of, quads, place = (jnp.asarray(a, BF) for a in (out_of, quads, place))
    vmem = pltpu.VMEM
    fine, coarse = pl.pallas_call(
        kernel,
        out_shape=(jax.ShapeDtypeStruct((864, D), BF), jax.ShapeDtypeStruct((3, 3, 6, 2048), BF)),
        in_specs=[pl.BlockSpec(memory_space=pl.ANY)] * 12,
        out_specs=(pl.BlockSpec(memory_space=pl.ANY),) * 2,
        scratch_shapes=[
            vmem((864, D), BF), vmem((96, 384), jnp.int32), vmem((2, D, 3 * D), BF), vmem((2, D, D), BF),
            vmem((2, D, FF), BF), vmem((2, FF, D), BF), vmem((4 * D, 2 * D), BF), vmem((4, 4096, 128), BF),
            vmem((512, 432), BF), vmem((432, 512), BF), vmem((1024, 1024), BF), vmem((1024, 256), BF),
            vmem((5, 5, CELL, D), BF), vmem((7, CELL, D), BF), vmem((5, WIN, WIN), F32),
            vmem((WIN, 3 * D), BF), vmem((WIN, D), BF), vmem((WIN, D), BF), vmem((WIN, D), F32), vmem((256, 2048), BF),
            vmem((2, 64, 4096), BF), vmem((4, 32, 4096), BF), vmem((4, 64, 128), BF), vmem((4, 64, 128), BF), vmem((4, 64, 128), BF),
            vmem((4, 4, 32, 128), BF), vmem((4, 4, 32, 128), BF),
            vmem((864, D), BF), vmem((64, 2048), F32), vmem((3, 3, 6, 2048), BF),
            pltpu.SemaphoreType.DMA((16,)), pltpu.SemaphoreType.DMA((2,)),
            pltpu.SemaphoreType.DMA((10,)), pltpu.SemaphoreType.DMA((10,)),
            pltpu.SemaphoreType.DMA((26,)), pltpu.SemaphoreType.DMA((26,)),
        ],
        compiler_params=pltpu.CompilerParams(
            collective_id=0, has_side_effects=True, vmem_limit_bytes=60 * 1024 * 1024
        ),
    )(
        tokens.reshape(864, D), region_ids, w_qkv, w_proj, w_up, w_down, merge_first, merge_second,
        out_of.T, out_of, quads, place,
    )
    specs = (pl.BlockSpec((288, D), lambda k: (k, 0)), pl.BlockSpec((1, 3, 6, 2048), lambda k: (k, 0, 0, 0)))
    fine, coarse = pl.pallas_call(
        hand_over,
        grid=(3,),
        out_shape=(jax.ShapeDtypeStruct(fine.shape, BF), jax.ShapeDtypeStruct(coarse.shape, BF)),
        in_specs=list(specs),
        out_specs=specs,
    )(fine, coarse)
    return fine.reshape(3, 12, 24, D), coarse


def solution(mesh):
    in_specs = (P(None, "lat", "lon", None), P(), P(), P(), P(), P(), P(), P(None, "lon"))
    out_specs = (P(None, "lat", "lon", None), P(None, "lat", "lon", None))
    return jax.shard_map(shards, mesh=mesh, in_specs=in_specs, out_specs=out_specs, check_vma=False)
```
